32 devices in a mesh: parts: 2 (over y), warp: 4 (over z), weft: 2 (over x), ply: 2 (over core).
Axes of the slice: x: 2, y: 2, z: 4, core: 2. Of those that a mesh axis runs over, the one named last changes fastest.
Arguments:
- lam_start: float32 [64, 256, 512], P(('parts', 'warp', 'ply'), 'weft'), parts along dimension 0, as said below
- resid_start: float32 [64, 256, 512], P(('parts', 'warp', 'ply'), 'weft'), parts along dimension 0, as said below
- dirn_start: float32 [64, 256, 512], P(('parts', 'warp', 'ply'), 'weft'), parts along dimension 0, as said below
- rz_start: float32 [2], P('parts'), parts along dimension 0, may hold values from 10485760 to 83886080
- pattern: int32 [64, 256], P(('parts', 'warp', 'ply'), 'weft'), parts along dimension 0, may hold values from 0 to 2
- corners: int32 [4, 64, 256], P(None, ('parts', 'warp', 'ply'), 'weft'), parts along dimension 1, may hold values from -1 to 127, as said below
- schur_inv: float32 [3, 512, 512], replicated, as said below
- schur_dirichlet: float32 [3, 512, 512], replicated, as said below
- corner_shape: float32 [3, 4, 512], replicated, may hold values from -0.3 to 0.3
- coarse_inv: float32 [256, 128], P(('parts', 'warp', 'weft', 'ply')), parts along dimension 0, as said below
Outputs:
- lam_final: float32 [64, 256, 512], P(('parts', 'warp', 'ply'), 'weft'), parts along dimension 0
- resid_final: float32 [64, 256, 512], P(('parts', 'warp', 'ply'), 'weft'), parts along dimension 0
- dirn_final: float32 [64, 256, 512], P(('parts', 'warp', 'ply'), 'weft'), parts along dimension 0
The draws below stay inside these ranges and needn't reach their ends.
There are 2 independent parts, one for each index of `parts`. The reference program is written for one: setup_inputs(seed, part) draws one part's arguments, and reference() takes and returns one part's arrays. A program takes and returns all parts, laid end to end along the dimension named above; an argument that names none is the same for every part. Nothing has to cross between parts.
Inputs may be any that keep to these rules, and one draw needn't show every extreme that they name: `lam_start`: in each cell the W block is minus the E block of the cell to its west and zero where j = 0; the S block is minus the N block of the cell to its south and zero where i = 0. `resid_start`: in each cell the W block is minus the E block of the cell to its west and zero where j = 0; the S block is minus the N block of the cell to its south and zero where i = 0. `dirn_start`: in each cell the W block is minus the E block of the cell to its west and zero where j = 0; the S block is minus the N block of the cell to its south and zero where i = 0. `corners`: corner k of cell (i, j) is the corner node (i, j), (i, j + 1), (i + 1, j) or (i + 1, j + 1) for k = 0, 1, 2, 3; nodes (a, b) with a = 32 or b = 256 are -1; every other node's row is that of its aggregate, the block of 8 x 8 nodes with the same a // 8 and b // 8; each aggregate has its own row, and which aggregate has which row is drawn. `schur_inv`: each matrix is symmetric positive definite. `schur_dirichlet`: each matrix is symmetric positive definite. `coarse_inv`: symmetric positive definite.
All inputs are finite; a program needn't handle non-finite values.
Results may differ from the reference program's by a relative error of at most 0.00027.
Values sent between devices are 32-bit elements; how exact they have to be, the bound alone decides.
A program may use at most 64 MiB of HBM per device.

```python
import math
import jax
import jax.numpy as jnp
from jax import lax

EDGE = 128
DOF = 512
NPAT = 3
ITERS = 3
AGG = 8
NR = 32
NC = 256
NCOARSE = 128


def base_values(key, shape):
    return jax.random.normal(key, shape, jnp.float32)


def redundant_field(key, spread):
    owned = base_values(key, (NR, NC, 2, EDGE)) * spread[:, :, None, None]
    east_side = owned[:, :, 0]
    north_side = owned[:, :, 1]
    zero_column = jnp.zeros((NR, 1, EDGE), jnp.float32)
    zero_row = jnp.zeros((1, NC, EDGE), jnp.float32)
    west_side = -jnp.concatenate([zero_column, east_side[:, :-1]], axis=1)
    south_side = -jnp.concatenate([zero_row, north_side[:-1]], axis=0)
    return jnp.concatenate([west_side, east_side, south_side, north_side], axis=2)


def draw_lam_start(key, part):
    return redundant_field(jax.random.fold_in(key, 11), jnp.ones((NR, NC), jnp.float32))


def draw_dirn_start(key, part):
    return redundant_field(jax.random.fold_in(key, 12), jnp.ones((NR, NC), jnp.float32))


def draw_resid_start(key, part):
    row_rise = 1.0 + jnp.arange(NR, dtype=jnp.float32)[:, None] / (NR - 1)
    col_rise = 1.0 + jnp.arange(NC, dtype=jnp.float32)[None, :] / (NC - 1)
    low_end, high_end = (0.4, 1.6)
    cell_scale = jnp.exp(jax.random.uniform(jax.random.fold_in(key, 14), (NR, NC), jnp.float32, math.log(low_end), math.log(high_end)))
    return redundant_field(jax.random.fold_in(key, 13), row_rise * col_rise * cell_scale)


def draw_corners(key, part):
    block_cols = NC // AGG
    block_count = NR // AGG * block_cols
    labels = jax.random.permutation(jax.random.fold_in(key, 31), block_count).astype(jnp.int32)
    node_row = jnp.arange(NR, dtype=jnp.int32)[:, None] // AGG
    node_col = jnp.arange(NC, dtype=jnp.int32)[None, :] // AGG
    block_index = node_row * block_cols + node_col
    table = labels[block_index].astype(jnp.int32)
    padded = jnp.full((NR + 1, NC + 1), -1, jnp.int32).at[:NR, :NC].set(table)
    return jnp.stack([padded[:-1, :-1], padded[:-1, 1:], padded[1:, :-1], padded[1:, 1:]], axis=0)


def spd_matrices(key, mat_count, dim_len, diag_low, diag_high, off_scale):
    off_raw = base_values(jax.random.fold_in(key, 1), (mat_count, dim_len, dim_len)) * (off_scale / math.sqrt(dim_len))
    symmetric = (off_raw + jnp.swapaxes(off_raw, 1, 2)) * 0.70710678
    diagonal = jax.random.uniform(jax.random.fold_in(key, 2), (mat_count, dim_len), jnp.float32, diag_low, diag_high)
    row_index = jnp.arange(dim_len)[:, None]
    col_index = jnp.arange(dim_len)[None, :]
    on_diag = (row_index == col_index).astype(jnp.float32)
    return symmetric * (1.0 - on_diag) + on_diag * diagonal[:, :, None]


def draw_schur_inv(key, part):
    return spd_matrices(jax.random.fold_in(key, 21), NPAT, DOF, 0.8, 1.6, 0.3)


def draw_schur_dirichlet(key, part):
    return spd_matrices(jax.random.fold_in(key, 22), NPAT, DOF, 2.0, 4.0, 0.8)


def draw_coarse_inv(key, part):
    level = 1.6 / math.sqrt(NR * NC / NCOARSE)
    return spd_matrices(jax.random.fold_in(key, 23), 1, NCOARSE, level, 2.0 * level, 0.3 * level)[0]


def plant(values, rng, least, top_value):
    longest = values.shape.index(max(values.shape))
    spots = []
    for shift in (0, 1):
        where = [jax.random.randint(jax.random.fold_in(rng, axis), (), 0, length) for axis, length in enumerate(values.shape)]
        where[longest] = (where[longest] + shift) % values.shape[longest]
        spots.append(tuple(where))
    return values.at[spots[0]].set(least).at[spots[1]].set(top_value)


def normal_values(own_key, shape, width, reach, held_as=jnp.bfloat16):
    values = width * jax.random.normal(own_key, shape, jnp.float32)
    return jnp.clip(values, min=-reach, max=reach).astype(held_as)


def setup_inputs(seed: int = 0, part: int = 0) -> dict:
    seeds = jax.random.split(jax.random.key(seed), 11)
    part_splits = jax.random.split(jax.random.fold_in(seeds[10], part), 11)
    return {
        "lam_start": draw_lam_start(jax.random.fold_in(jax.random.fold_in(seeds[10], part), 71), part),
        "resid_start": draw_resid_start(jax.random.fold_in(jax.random.fold_in(seeds[10], part), 71), part),
        "dirn_start": draw_dirn_start(jax.random.fold_in(jax.random.fold_in(seeds[10], part), 71), part),
        "rz_start": jnp.clip(jnp.exp(jax.random.uniform(part_splits[3], (1,), jnp.float32, math.log(10485760), math.log(83886080))), 10485760, 83886080),
        "pattern": plant(jax.random.randint(part_splits[4], (NR, NC), 0, NPAT), jax.random.fold_in(part_splits[4], 1), 0, NPAT - 1).astype(jnp.int32),
        "corners": draw_corners(jax.random.fold_in(jax.random.fold_in(seeds[10], part), 71), part),
        "schur_inv": draw_schur_inv(jax.random.fold_in(seeds[10], 71), part),
        "schur_dirichlet": draw_schur_dirichlet(jax.random.fold_in(seeds[10], 71), part),
        "corner_shape": normal_values(seeds[8], (NPAT, 4, DOF), 0.05, 0.3, jnp.float32),
        "coarse_inv": draw_coarse_inv(jax.random.fold_in(jax.random.fold_in(seeds[10], part), 71), part),
    }


HIGHEST = lax.Precision.HIGHEST


def split_edges(values):
    return (values[..., :EDGE], values[..., EDGE:2 * EDGE], values[..., 2 * EDGE:3 * EDGE], values[..., 3 * EDGE:])


def cross_faces(values, west_keep, south_keep):
    west_side, east_side, south_side, north_side = split_edges(values)
    zero_column = jnp.zeros((NR, 1, EDGE), values.dtype)
    zero_row = jnp.zeros((1, NC, EDGE), values.dtype)
    east_west = jnp.concatenate([west_side[:, 1:], zero_column], axis=1)
    west_east = jnp.concatenate([zero_column, east_side[:, :-1]], axis=1)
    north_south = jnp.concatenate([south_side[1:], zero_row], axis=0)
    south_north = jnp.concatenate([zero_row, north_side[:-1]], axis=0)
    return jnp.concatenate([(west_side - west_east) * west_keep, east_side - east_west, (south_side - south_north) * south_keep, north_side - north_south], axis=2)


def apply_cells(values, matrices, selector):
    rows_flat = values.reshape(-1, DOF)
    result = jnp.zeros_like(rows_flat)
    for pattern_id in range(NPAT):
        product = jnp.dot(rows_flat, matrices[pattern_id], precision=HIGHEST, preferred_element_type=jnp.float32)
        result = result + selector[pattern_id][:, None] * product
    return result


def reference(lam_start, resid_start, dirn_start, rz_start, pattern, corners, schur_inv, schur_dirichlet, corner_shape, coarse_inv):
    float_type = lam_start.dtype
    row_pos = lax.broadcasted_iota(jnp.int32, (NR, NC, 1), 0)
    col_pos = lax.broadcasted_iota(jnp.int32, (NR, NC, 1), 1)
    west_keep = (col_pos > 0).astype(float_type)
    south_keep = (row_pos > 0).astype(float_type)
    east_weight = jnp.where(col_pos == NC - 1, 1.0, 0.5).astype(float_type)
    north_weight = jnp.where(row_pos == NR - 1, 1.0, 0.5).astype(float_type)
    block_shape = (NR, NC, EDGE)
    edge_weight = jnp.concatenate([jnp.broadcast_to(0.5 * west_keep, block_shape), jnp.broadcast_to(east_weight, block_shape), jnp.broadcast_to(0.5 * south_keep, block_shape), jnp.broadcast_to(north_weight, block_shape)], axis=2)
    cell_kind = pattern.reshape(-1).astype(jnp.int32)
    selector = (cell_kind[None, :] == jnp.arange(NPAT, dtype=jnp.int32)[:, None]).astype(float_type)
    corner_rows = corners.reshape(4, -1).astype(jnp.int32)
    corner_live = corner_rows >= 0
    corner_slot = jnp.where(corner_live, corner_rows, NCOARSE).astype(jnp.int32)
    corner_pick = jnp.where(corner_live, corner_rows, 0).astype(jnp.int32)
    multiplier, residual, direction = lam_start, resid_start, dirn_start
    rz_prev = rz_start[0]
    for iteration in range(ITERS):
        spread = apply_cells(edge_weight * residual, schur_dirichlet, selector).reshape(NR, NC, DOF)
        precond = edge_weight * cross_faces(spread, west_keep, south_keep)
        rz_now = jnp.sum(edge_weight * residual * precond)
        direction = precond + (rz_now / rz_prev) * direction
        rows_flat = direction.reshape(-1, DOF)
        local_image = apply_cells(direction, schur_inv, selector)
        corner_terms = jnp.einsum("pkd,cd->pkc", corner_shape, rows_flat, precision=HIGHEST)
        corner_load = jnp.sum(corner_terms * selector[:, None, :], axis=0)
        coarse_rhs = jax.ops.segment_sum(corner_load.reshape(-1), corner_slot.reshape(-1), num_segments=NCOARSE + 1)[:NCOARSE]
        coarse_sol = jnp.dot(coarse_inv, coarse_rhs, precision=HIGHEST)
        corner_vals = jnp.where(corner_live, coarse_sol[corner_pick], 0.0)
        full_image = local_image + jnp.einsum("pkc,pkd->cd", selector[:, None, :] * corner_vals[None], corner_shape, precision=HIGHEST)
        applied = cross_faces(full_image.reshape(NR, NC, DOF), west_keep, south_keep)
        curvature = jnp.sum(edge_weight * direction * applied)
        alpha_step = rz_now / curvature
        multiplier = multiplier + alpha_step * direction
        residual = residual - alpha_step * applied
        rz_prev = rz_now
    return multiplier, residual, direction
```

```python
import functools

import jax
import jax.numpy as jnp
from jax import lax
from jax.experimental import pallas as pl
from jax.experimental.pallas import tpu as pltpu
from jax.sharding import PartitionSpec as P

ITERS = 3
HIGHEST = lax.Precision.HIGHEST
F32 = jnp.float32
BF16 = jnp.bfloat16
MESH = pl.DeviceIdType.MESH
NN = (((1,), (0,)), ((), ()))
NT = (((1,), (1,)), ((), ()))
TN = (((0,), (0,)), ((), ()))


def dot(a, b, dims=NN):
    return lax.dot_general(a, b, dims, preferred_element_type=F32)


def split2(x):
    hi = x.astype(BF16)
    return hi, (x - hi.astype(F32)).astype(BF16)


def split3(x):
    hi = x.astype(BF16).astype(F32)
    rest = x - hi
    mid = rest.astype(BF16).astype(F32)
    return hi, mid, rest - mid


def kernel(
    nw, nf, npl, rows, cols, edge, npat, ncoarse,
    lam_in, res_in, dir_in, rz_in, pat, cor, sinv, sdir, shp, cinv,
    lam, res, dirn,
    m_hi, m_lo, x_hi, x_lo, masks, field, info, infosend, oht, sel, shape_f, shape_st,
    ginv, rz_slots, cv_slots, co_slots, rzprev,
    hns_send, hns_recv, hew_send, hew_recv,
    h_ssem, h_rsem, i_ssem, i_rsem, a_ssem, a_rsem,
):
    n = nw * nf * npl
    cells = rows * cols
    dof = 4 * edge
    warp, weft, ply = lax.axis_index("warp"), lax.axis_index("weft"), lax.axis_index("ply")
    me = (warp * nf + weft) * npl + ply
    tile = warp * npl + ply
    ntile = nw * npl
    has_n, has_s = tile < ntile - 1, tile > 0
    has_e, has_w = weft < nf - 1, weft > 0
    north = {"warp": (tile + 1) // npl, "ply": (tile + 1) % npl, "weft": weft}
    south = {"warp": (tile + ntile - 1) // npl % nw, "ply": (tile + npl - 1) % npl, "weft": weft}
    east = {"warp": warp, "ply": ply, "weft": weft + 1}
    west = {"warp": warp, "ply": ply, "weft": weft - 1}

    def peer(t):
        other = lax.rem(me + t, n)
        return {"warp": other // (nf * npl), "weft": other // npl % nf, "ply": other % npl}

    B_S, B_N, B_W, B_E = (cells + k * cols for k in range(4))

    for k in range(4):
        for i in range(rows):
            info[k : k + 1, i * cols : (i + 1) * cols] = cor[k, i : i + 1, :].astype(F32)
    for i in range(rows):
        info[4:5, i * cols : (i + 1) * cols] = pat[i : i + 1, :].astype(F32)
    info[5:8, 0:cells] = jnp.zeros((3, cells), F32)
    for there, lane in ((has_s, B_S), (has_n, B_N), (has_w, B_W), (has_e, B_E)):
        @pl.when(jnp.logical_not(there))
        def _():
            info[:, lane : lane + cols] = jnp.full((8, cols), -1.0, F32)
    for there, k in ((has_s, 0), (has_n, 1)):
        @pl.when(jnp.logical_not(there))
        def _():
            hns_recv[:, k] = jnp.zeros((2 * ITERS, cols, edge), F32)
    for there, k in ((has_w, 0), (has_e, 1)):
        @pl.when(jnp.logical_not(there))
        def _():
            hew_recv[:, k] = jnp.zeros((2 * ITERS, 8, edge), F32)
    own = info[:, 0:cells]
    infosend[0] = own[:, (rows - 1) * cols :]
    infosend[1] = own[:, :cols]
    cell_i = lax.broadcasted_iota(jnp.int32, (cells, cols), 0)
    lane_i = lax.broadcasted_iota(jnp.int32, (cells, cols), 1)
    for slot, j in ((2, cols - 1), (3, 0)):
        pick = jnp.where(cell_i == lane_i * cols + j, 1.0, 0.0).astype(F32)
        infosend[slot] = lax.dot_general(
            own, pick, NN, precision=HIGHEST, preferred_element_type=F32
        )
    ginv[me] = cinv[...]

    barrier = pltpu.get_barrier_semaphore()

    def greet(t, c):
        pl.semaphore_signal(barrier, inc=1, device_id=peer(t), device_id_type=MESH)
        return c

    lax.fori_loop(1, n, greet, 0)
    pl.semaphore_wait(barrier, n - 1)

    def send_all(ref, src, which):
        def one(t, c):
            pltpu.make_async_remote_copy(
                src_ref=src, dst_ref=src, send_sem=a_ssem.at[which], recv_sem=a_rsem.at[which],
                device_id=peer(t), device_id_type=MESH,
            ).start()
            return c

        lax.fori_loop(1, n, one, 0)

    def wait_all(ref, sem):
        pltpu.make_async_copy(ref, ref, sem).wait()

    send_all(None, ginv.at[me], 3 * ITERS)

    def put(src, dst, ssem, rsem, to):
        return pltpu.make_async_remote_copy(
            src_ref=src, dst_ref=dst, send_sem=ssem, recv_sem=rsem,
            device_id=to, device_id_type=MESH,
        )

    def info_copies():
        return (
            (has_n, has_s, put(infosend.at[0], info.at[:, B_S : B_S + cols], i_ssem.at[0], i_rsem.at[0], north)),
            (has_s, has_n, put(infosend.at[1], info.at[:, B_N : B_N + cols], i_ssem.at[1], i_rsem.at[1], south)),
            (has_e, has_w, put(infosend.at[2], info.at[:, B_W : B_W + cols], i_ssem.at[2], i_rsem.at[2], east)),
            (has_w, has_e, put(infosend.at[3], info.at[:, B_E : B_E + cols], i_ssem.at[3], i_rsem.at[3], west)),
        )

    def halo_copies(ph):
        return (
            (has_n, has_s, put(hns_send.at[ph, 0], hns_recv.at[ph, 0], h_ssem.at[ph, 0], h_rsem.at[ph, 0], north)),
            (has_s, has_n, put(hns_send.at[ph, 1], hns_recv.at[ph, 1], h_ssem.at[ph, 1], h_rsem.at[ph, 1], south)),
            (has_e, has_w, put(hew_send.at[ph, 0], hew_recv.at[ph, 0], h_ssem.at[ph, 2], h_rsem.at[ph, 2], east)),
            (has_w, has_e, put(hew_send.at[ph, 1], hew_recv.at[ph, 1], h_ssem.at[ph, 3], h_rsem.at[ph, 3], west)),
        )

    def start_copies(copies):
        for out, _, copy in copies:
            @pl.when(out)
            def _(copy=copy):
                copy.start()

    def wait_recv(copies):
        for _, came, copy in copies:
            @pl.when(came)
            def _(copy=copy):
                copy.wait_recv()

    def wait_send(copies):
        for out, _, copy in copies:
            @pl.when(out)
            def _(copy=copy):
                copy.wait_send()

    start_copies(info_copies())

    for src, which in ((sdir, 0), (sinv, 1)):
        for p in range(npat):
            hi, lo = split2(src[p])
            m_hi[which, p * dof : (p + 1) * dof, :] = hi
            m_lo[which, p * dof : (p + 1) * dof, :] = lo
    prow = lax.broadcasted_iota(jnp.int32, (8, cells), 0).astype(F32)
    onehot = jnp.where(prow == own[4:5, :], 1.0, 0.0).astype(F32)
    for p in range(npat):
        spread_p = jnp.where(lax.broadcasted_iota(jnp.int32, (8, edge), 0) == p, 1.0, 0.0)
        masks[p] = dot(onehot.astype(BF16), spread_p.astype(BF16), TN).astype(BF16)
    shape_f[...] = jnp.zeros_like(shape_f)
    for p in range(npat):
        shape_f[4 * p : 4 * p + 4, :] = shp[p]
    s_hi, s_lo = split2(shape_f[...])
    shape_st[0:16, :] = s_hi
    shape_st[16:32, :] = s_hi
    shape_st[32:48, :] = s_lo
    lam[...] = lam_in[...]
    res[...] = res_in[...]
    dirn[...] = dir_in[...]
    rzprev[...] = jnp.broadcast_to(rz_in[...], rzprev.shape)

    wait_recv(info_copies())
    ext = cells + 4 * cols
    row_k = lax.broadcasted_iota(jnp.int32, (16, ext), 0)
    sel[...] = jnp.where((row_k // 4).astype(F32) == info[4:5, :], 1.0, 0.0)
    coarse_row = lax.broadcasted_iota(jnp.int32, (ncoarse, ext), 0).astype(F32)
    for k in range(4):
        oht[k] = jnp.where(coarse_row == info[k : k + 1, :], 1.0, 0.0).astype(BF16)

    sub = lax.broadcasted_iota(jnp.int32, (cols, edge), 0)
    first, final = sub == 0, sub == cols - 1
    w_east = jnp.where(final & jnp.logical_not(has_e), 1.0, 0.5)
    no_w = first & jnp.logical_not(has_w)
    w_north = jnp.where(has_n, 0.5, 1.0)
    keep_s = jnp.where(has_s, 1.0, 0.0)
    BW, BE, BS, BN = (slice(b * edge, (b + 1) * edge) for b in range(4))

    def rowslice(i):
        return slice(i * cols, (i + 1) * cols)

    def set_operand(i, b, x):
        hi, lo = split2(x)
        for p in range(npat):
            m = masks[p, rowslice(i), :]
            x_hi[rowslice(i), p * dof + b * edge : p * dof + (b + 1) * edge] = hi * m
            x_lo[rowslice(i), p * dof + b * edge : p * dof + (b + 1) * edge] = lo * m

    def product(which):
        xh = x_hi[...]
        return dot(xh, m_hi[which]) + (dot(x_lo[...], m_hi[which]) + dot(xh, m_lo[which]))

    def send_halo(ph):
        hns_send[ph, 0] = field[rowslice(rows - 1), BN]
        hns_send[ph, 1] = field[rowslice(0), BS]
        for i in range(rows):
            hew_send[ph, 0, i : i + 1, :] = field[(i + 1) * cols - 1 : (i + 1) * cols, BE]
            hew_send[ph, 1, i : i + 1, :] = field[i * cols : i * cols + 1, BW]
        start_copies(halo_copies(ph))

    def fold(x):
        return jnp.sum(x.reshape(-1, 8, x.shape[-1]), axis=0)

    def lanes(x):
        total = x[:, :edge]
        for b in range(1, x.shape[1] // edge):
            total = total + x[:, b * edge : (b + 1) * edge]
        return total

    def jump(i, b, hs, hn, hw, he):
        r = rowslice(i)
        if b == 0:
            other = jnp.where(first, hw[i : i + 1, :], pltpu.roll(field[r, BE], 1, 0))
            return jnp.where(no_w, 0.0, field[r, BW] - other)
        if b == 1:
            other = jnp.where(final, he[i : i + 1, :], pltpu.roll(field[r, BW], cols - 1, 0))
            return field[r, BE] - other
        if b == 2:
            if i == 0:
                return (field[r, BS] - hs) * keep_s
            return field[r, BS] - field[rowslice(i - 1), BN]
        if i == rows - 1:
            return field[r, BN] - hn
        return field[r, BN] - field[rowslice(i + 1), BS]

    def weight(i, b):
        if b == 1:
            return w_east
        if b == 3 and i == rows - 1:
            return w_north
        return 0.5

    def total(ref):
        return jnp.sum(ref, axis=(0, 1, 2), keepdims=False)

    def everywhere(slots):
        part = jnp.sum(slots, axis=0)
        return jnp.sum(jnp.sum(part, axis=1, keepdims=True), axis=0, keepdims=True)

    rk = lax.broadcasted_iota(jnp.int32, (16, ext), 0) % 4
    rk_c = lax.broadcasted_iota(jnp.int32, (16, ncoarse), 0) % 4

    def body(it, carry):
        pa, pb = 2 * it, 2 * it + 1
        for i in range(rows):
            for b in range(4):
                set_operand(i, b, weight(i, b) * res[rowslice(i), b * edge : (b + 1) * edge])
        field[...] = product(0)
        send_halo(pa)
        acc = jnp.zeros((8, edge), F32)
        for i in range(rows):
            for b in range(4):
                bs = slice(b * edge, (b + 1) * edge)
                acc = acc + fold(weight(i, b) * res[rowslice(i), bs] * field[rowslice(i), bs])
        rz_slots[it, me] = acc
        send_all(None, rz_slots.at[it, me], 3 * it)
        wait_recv(halo_copies(pa))
        wait_all(rz_slots.at[it, pl.ds(0, n - 1)], a_rsem.at[3 * it])
        rz_now = everywhere(rz_slots[it])
        beta = rz_now / rzprev[0:1, 0:1]
        hs, hn = hns_recv[pa, 0], hns_recv[pa, 1]
        hw, he = hew_recv[pa, 0], hew_recv[pa, 1]
        for i in range(rows):
            for b in range(4):
                bs = slice(b * edge, (b + 1) * edge)
                d = weight(i, b) * jump(i, b, hs, hn, hw, he) + beta * dirn[rowslice(i), bs]
                dirn[rowslice(i), bs] = d
                set_operand(i, b, d)
        d_hi, d_lo = split2(dirn[...])
        terms = dot(s_hi, d_hi, NT) + (dot(s_lo, d_hi, NT) + dot(s_hi, d_lo, NT))
        terms = terms * sel[:, 0:cells]
        stack = jnp.concatenate(split3(terms), axis=0).astype(BF16)
        load = jnp.zeros((16, ncoarse), F32)
        for k in range(4):
            r = dot(stack, oht[k, :, 0:cells], NT)
            load = load + jnp.where(rk_c == k, r[0:16] + r[16:32] + r[32:48], 0.0)
        co_slots[it, me] = load[0:8] + load[8:16]
        send_all(None, co_slots.at[it, me], 3 * it + 1)
        field[...] = product(1)
        send_halo(pb)
        cv_slots[it, me] = lanes(fold(dirn[...] * field[...]))
        send_all(None, cv_slots.at[it, me], 3 * it + 2)

        @pl.when(it == 0)
        def _():
            wait_all(ginv.at[pl.ds(0, n - 1)], a_rsem.at[3 * ITERS])

        wait_all(co_slots.at[it, pl.ds(0, n - 1)], a_rsem.at[3 * it + 1])
        rhs = jnp.sum(jnp.sum(co_slots[it], axis=0), axis=0, keepdims=True)
        rhs = jnp.broadcast_to(rhs, (8, ncoarse))
        sol = lax.dot_general(
            rhs, ginv[...].reshape(ncoarse, ncoarse), NT, precision=HIGHEST,
            preferred_element_type=F32,
        )
        hi, mid, lo = split3(sol)
        srow = lax.broadcasted_iota(jnp.int32, (8, ncoarse), 0)
        lhs = jnp.where(srow == 0, hi, jnp.where(srow == 1, mid, jnp.where(srow == 2, lo, 0.0)))
        lhs = jnp.concatenate([lhs, jnp.zeros_like(lhs)], axis=0).astype(BF16)
        vals = jnp.zeros((16, ext), F32)
        for k in range(4):
            cv = jnp.sum(dot(lhs, oht[k]), axis=0, keepdims=True)
            vals = jnp.where(rk == k, cv, vals)
        a_hi, a_lo = split2(vals * sel[...])
        a_st = jnp.concatenate([a_hi, a_lo, a_hi], axis=0)
        field[...] = field[...] + dot(a_st[:, 0:cells], shape_st[...], TN)
        add_s = dot(a_st[:, B_S : B_S + cols], shape_st[:, BN], TN)
        add_n = dot(a_st[:, B_N : B_N + cols], shape_st[:, BS], TN)
        add_w = dot(a_st[:, B_W : B_W + cols], shape_st[:, BE], TN)
        add_e = dot(a_st[:, B_E : B_E + cols], shape_st[:, BW], TN)
        wait_recv(halo_copies(pb))
        hs, hn = hns_recv[pb, 0] + add_s, hns_recv[pb, 1] + add_n
        hw, he = hew_recv[pb, 0] + add_w[0:8], hew_recv[pb, 1] + add_e[0:8]
        wait_all(cv_slots.at[it, pl.ds(0, n - 1)], a_rsem.at[3 * it + 2])
        curvature = everywhere(cv_slots[it]) + jnp.sum(
            sol[0:1] * rhs[0:1], axis=1, keepdims=True
        )
        alpha = rz_now / curvature
        for i in range(rows):
            for b in range(4):
                bs = slice(b * edge, (b + 1) * edge)
                rs = rowslice(i)
                lam[rs, bs] = lam[rs, bs] + alpha * dirn[rs, bs]
                res[rs, bs] = res[rs, bs] - alpha * jump(i, b, hs, hn, hw, he)
        rzprev[...] = jnp.broadcast_to(rz_now, rzprev.shape)
        return carry

    lax.fori_loop(0, ITERS, body, 0)

    wait_send(info_copies())
    wait_all(ginv.at[pl.ds(0, n - 1)], a_ssem.at[3 * ITERS])
    for it in range(ITERS):
        wait_send(halo_copies(2 * it))
        wait_send(halo_copies(2 * it + 1))
        wait_all(rz_slots.at[it, pl.ds(0, n - 1)], a_ssem.at[3 * it])
        wait_all(co_slots.at[it, pl.ds(0, n - 1)], a_ssem.at[3 * it + 1])
        wait_all(cv_slots.at[it, pl.ds(0, n - 1)], a_ssem.at[3 * it + 2])


def on_device(
    lam_start, resid_start, dirn_start, rz_start, pattern, corners,
    schur_inv, schur_dirichlet, corner_shape, coarse_inv,
):
    rows, cols, dof = lam_start.shape
    edge = dof // 4
    npat = schur_inv.shape[0]
    ncoarse = coarse_inv.shape[1]
    nw, nf, npl = lax.axis_size("warp"), lax.axis_size("weft"), lax.axis_size("ply")
    n = nw * nf * npl
    cells = rows * cols
    ext = cells + 4 * cols
    vmem = pl.BlockSpec(memory_space=pltpu.VMEM)
    out = jax.ShapeDtypeStruct((cells, dof), F32)
    V = pltpu.VMEM
    D = pltpu.SemaphoreType.DMA
    outs = pl.pallas_call(
        functools.partial(kernel, nw, nf, npl, rows, cols, edge, npat, ncoarse),
        out_shape=(out, out, out),
        in_specs=[vmem] * 10,
        out_specs=(vmem, vmem, vmem),
        scratch_shapes=[
            V((2, npat * dof, dof), BF16),
            V((2, npat * dof, dof), BF16),
            V((cells, npat * dof), BF16),
            V((cells, npat * dof), BF16),
            V((npat, cells, edge), BF16),
            V((cells, dof), F32),
            V((8, ext), F32),
            V((4, 8, cols), F32),
            V((4, ncoarse, ext), BF16),
            V((16, ext), F32),
            V((16, dof), F32),
            V((48, dof), BF16),
            V((n, ncoarse // n, ncoarse), F32),
            V((ITERS, n, 8, edge), F32),
            V((ITERS, n, 8, edge), F32),
            V((ITERS, n, 8, ncoarse), F32),
            V((8, 128), F32),
            V((2 * ITERS, 2, cols, edge), F32),
            V((2 * ITERS, 2, cols, edge), F32),
            V((2 * ITERS, 2, 8, edge), F32),
            V((2 * ITERS, 2, 8, edge), F32),
            D((2 * ITERS, 4)),
            D((2 * ITERS, 4)),
            D((4,)),
            D((4,)),
            D((3 * ITERS + 1,)),
            D((3 * ITERS + 1,)),
        ],
        compiler_params=pltpu.CompilerParams(
            collective_id=0, has_side_effects=True, vmem_limit_bytes=60 * 1024 * 1024
        ),
    )(
        lam_start.reshape(cells, dof), resid_start.reshape(cells, dof),
        dirn_start.reshape(cells, dof), rz_start.reshape(1, 1), pattern, corners,
        schur_inv, schur_dirichlet, corner_shape, coarse_inv,
    )
    return tuple(o.reshape(rows, cols, dof) for o in outs)


def solution(mesh):
    field = P(("parts", "warp", "ply"), "weft", None)
    return jax.shard_map(
        on_device,
        mesh=mesh,
        in_specs=(
            field, field, field,
            P("parts"),
            P(("parts", "warp", "ply"), "weft"),
            P(None, ("parts", "warp", "ply"), "weft"),
            P(), P(), P(),
            P(("parts", "warp", "weft", "ply"), None),
        ),
        out_specs=(field, field, field),
        check_vma=False,
    )
```

```python
import functools

import jax
import jax.numpy as jnp
from jax import lax
from jax.experimental import pallas as pl
from jax.experimental.pallas import tpu as pltpu
from jax.sharding import PartitionSpec as P

ITERS = 3
HIGHEST = lax.Precision.HIGHEST
F32 = jnp.float32
BF16 = jnp.bfloat16
MESH = pl.DeviceIdType.MESH
NN = (((1,), (0,)), ((), ()))
NT = (((1,), (1,)), ((), ()))
TN = (((0,), (0,)), ((), ()))


def dot(a, b, dims=NN):
    return lax.dot_general(a, b, dims, preferred_element_type=F32)


def split2(x):
    hi = x.astype(BF16)
    return hi, (x - hi.astype(F32)).astype(BF16)


def split3(x):
    hi = x.astype(BF16).astype(F32)
    rest = x - hi
    mid = rest.astype(BF16).astype(F32)
    return hi, mid, rest - mid


def kernel(
    nw, nf, npl, rows, cols, edge, npat, ncoarse,
    lam_in, res_in, dir_in, rz_in, pat, cor, sinv, sdir, shp, cinv,
    lam, res, dirn,
    sdir_v, sinv_v, s_f, p_f, f_f, app, hp_ns, hp_ew, scal, crhs,
    m_hi, m_lo, x_hi, x_lo, masks, info, infosend, oht, sel, shape_f, shape_st,
    ginv, rz_slots, cv_slots, co_slots,
    hns_send, hns_recv, hew_send, hew_recv,
    h_ssem, h_rsem, i_ssem, i_rsem, a_ssem, a_rsem, l_sem,
):
    n = nw * nf * npl
    cells = rows * cols
    dof = 4 * edge
    warp, weft, ply = lax.axis_index("warp"), lax.axis_index("weft"), lax.axis_index("ply")
    me = (warp * nf + weft) * npl + ply
    tile = warp * npl + ply
    ntile = nw * npl
    has_n, has_s = tile < ntile - 1, tile > 0
    has_e, has_w = weft < nf - 1, weft > 0
    north = {"warp": (tile + 1) // npl, "ply": (tile + 1) % npl, "weft": weft}
    south = {"warp": (tile + ntile - 1) // npl % nw, "ply": (tile + npl - 1) % npl, "weft": weft}
    east = {"warp": warp, "ply": ply, "weft": weft + 1}
    west = {"warp": warp, "ply": ply, "weft": weft - 1}

    def peer(t):
        other = lax.rem(me + t, n)
        return {"warp": other // (nf * npl), "weft": other // npl % nf, "ply": other % npl}

    RZ, ALPHA, EARLY, LATE, CC = range(5)
    B_S, B_N, B_W, B_E = (cells + k * cols for k in range(4))

    barrier = pltpu.get_barrier_semaphore()

    def greet(t, c):
        pl.semaphore_signal(barrier, inc=1, device_id=peer(t), device_id_type=MESH)
        return c

    loads = [
        pltpu.make_async_copy(src, dst, l_sem.at[k])
        for k, (src, dst) in enumerate(
            ((sdir, sdir_v), (res_in, res), (dir_in, dirn), (sinv, sinv_v), (lam_in, lam))
        )
    ]
    for load in loads:
        load.start()

    for k in range(4):
        for i in range(rows):
            info[k : k + 1, i * cols : (i + 1) * cols] = cor[k, i : i + 1, :].astype(F32)
    for i in range(rows):
        info[4:5, i * cols : (i + 1) * cols] = pat[i : i + 1, :].astype(F32)
    info[5:8, 0:cells] = jnp.zeros((3, cells), F32)
    for there, lane in ((has_s, B_S), (has_n, B_N), (has_w, B_W), (has_e, B_E)):
        @pl.when(jnp.logical_not(there))
        def _():
            info[:, lane : lane + cols] = jnp.full((8, cols), -1.0, F32)
    for there, k in ((has_s, 0), (has_n, 1)):
        @pl.when(jnp.logical_not(there))
        def _():
            hns_recv[:, k] = jnp.zeros((2 * ITERS, cols, edge), F32)
    for there, k in ((has_w, 0), (has_e, 1)):
        @pl.when(jnp.logical_not(there))
        def _():
            hew_recv[:, k] = jnp.zeros((2 * ITERS, 8, edge), F32)
    own = info[:, 0:cells]
    infosend[0] = own[:, (rows - 1) * cols :]
    infosend[1] = own[:, :cols]
    cell_i = lax.broadcasted_iota(jnp.int32, (cells, cols), 0)
    lane_i = lax.broadcasted_iota(jnp.int32, (cells, cols), 1)
    for slot, j in ((2, cols - 1), (3, 0)):
        pick = jnp.where(cell_i == lane_i * cols + j, 1.0, 0.0).astype(F32)
        infosend[slot] = lax.dot_general(
            own, pick, NN, precision=HIGHEST, preferred_element_type=F32
        )
    ginv[me] = cinv[...]
    lax.fori_loop(1, n, greet, 0)

    def send_all(ref, src, which):
        def one(t, c):
            pltpu.make_async_remote_copy(
                src_ref=src, dst_ref=src, send_sem=a_ssem.at[which], recv_sem=a_rsem.at[which],
                device_id=peer(t), device_id_type=MESH,
            ).start()
            return c

        lax.fori_loop(1, n, one, 0)

    def wait_all(ref, sem):
        pltpu.make_async_copy(ref, ref, sem).wait()

    def put(src, dst, ssem, rsem, to):
        return pltpu.make_async_remote_copy(
            src_ref=src, dst_ref=dst, send_sem=ssem, recv_sem=rsem,
            device_id=to, device_id_type=MESH,
        )

    def info_copies():
        return (
            (has_n, has_s, put(infosend.at[0], info.at[:, B_S : B_S + cols], i_ssem.at[0], i_rsem.at[0], north)),
            (has_s, has_n, put(infosend.at[1], info.at[:, B_N : B_N + cols], i_ssem.at[1], i_rsem.at[1], south)),
            (has_e, has_w, put(infosend.at[2], info.at[:, B_W : B_W + cols], i_ssem.at[2], i_rsem.at[2], east)),
            (has_w, has_e, put(infosend.at[3], info.at[:, B_E : B_E + cols], i_ssem.at[3], i_rsem.at[3], west)),
        )

    def halo_copies(ph):
        return (
            (has_n, has_s, put(hns_send.at[ph, 0], hns_recv.at[ph, 0], h_ssem.at[ph, 0], h_rsem.at[ph, 0], north)),
            (has_s, has_n, put(hns_send.at[ph, 1], hns_recv.at[ph, 1], h_ssem.at[ph, 1], h_rsem.at[ph, 1], south)),
            (has_e, has_w, put(hew_send.at[ph, 0], hew_recv.at[ph, 0], h_ssem.at[ph, 2], h_rsem.at[ph, 2], east)),
            (has_w, has_e, put(hew_send.at[ph, 1], hew_recv.at[ph, 1], h_ssem.at[ph, 3], h_rsem.at[ph, 3], west)),
        )

    def start_copies(copies):
        for out, _, copy in copies:
            @pl.when(out)
            def _(copy=copy):
                copy.start()

    def wait_recv(copies):
        for _, came, copy in copies:
            @pl.when(came)
            def _(copy=copy):
                copy.wait_recv()

    def wait_send(copies):
        for out, _, copy in copies:
            @pl.when(out)
            def _(copy=copy):
                copy.wait_send()

    def split_matrices(src, which):
        for p in range(npat):
            hi, lo = split2(src[p])
            m_hi[which, p * dof : (p + 1) * dof, :] = hi
            m_lo[which, p * dof : (p + 1) * dof, :] = lo

    prow = lax.broadcasted_iota(jnp.int32, (8, cells), 0).astype(F32)
    onehot = jnp.where(prow == own[4:5, :], 1.0, 0.0).astype(F32)
    for p in range(npat):
        spread_p = jnp.where(lax.broadcasted_iota(jnp.int32, (8, edge), 0) == p, 1.0, 0.0)
        masks[p] = dot(onehot.astype(BF16), spread_p.astype(BF16), TN).astype(BF16)
    shape_f[...] = jnp.zeros_like(shape_f)
    for p in range(npat):
        shape_f[4 * p : 4 * p + 4, :] = shp[p]
    s_hi, s_lo = split2(shape_f[...])
    shape_st[0:16, :] = s_hi
    shape_st[16:32, :] = s_hi
    shape_st[32:48, :] = s_lo
    for ref in (s_f, p_f, hp_ns, hp_ew, crhs):
        ref[...] = jnp.zeros_like(ref)
    scal[RZ] = jnp.broadcast_to(rz_in[...], (8, edge))
    ext = cells + 4 * cols

    def coarse_tables():
        row_k = lax.broadcasted_iota(jnp.int32, (16, ext), 0)
        sel[...] = jnp.where((row_k // 4).astype(F32) == info[4:5, :], 1.0, 0.0)
        coarse_row = lax.broadcasted_iota(jnp.int32, (ncoarse, ext), 0).astype(F32)
        for k in range(4):
            oht[k] = jnp.where(coarse_row == info[k : k + 1, :], 1.0, 0.0).astype(BF16)

    sub = lax.broadcasted_iota(jnp.int32, (cols, edge), 0)
    first, final = sub == 0, sub == cols - 1
    w_east = jnp.where(final & jnp.logical_not(has_e), 1.0, 0.5)
    no_w = first & jnp.logical_not(has_w)
    w_north = jnp.where(has_n, 0.5, 1.0)
    keep_s = jnp.where(has_s, 1.0, 0.0)
    BW, BE, BS, BN = (slice(b * edge, (b + 1) * edge) for b in range(4))

    def rowslice(i):
        return slice(i * cols, (i + 1) * cols)

    def set_operand(i, b, x):
        hi, lo = split2(x)
        for p in range(npat):
            m = masks[p, rowslice(i), :]
            x_hi[rowslice(i), p * dof + b * edge : p * dof + (b + 1) * edge] = hi * m
            x_lo[rowslice(i), p * dof + b * edge : p * dof + (b + 1) * edge] = lo * m

    def product(which, half):
        xh = x_hi[...]
        hs = slice(half * 2 * edge, (half + 1) * 2 * edge)
        mh = m_hi[which, :, hs]
        return dot(xh, mh) + (dot(x_lo[...], mh) + dot(xh, m_lo[which, :, hs]))

    def send_ns(ph, field):
        hns_send[ph, 0] = field[rowslice(rows - 1), BN]
        hns_send[ph, 1] = field[rowslice(0), BS]
        start_copies(halo_copies(ph)[0:2])

    def send_ew(ph, field):
        for i in range(rows):
            hew_send[ph, 0, i : i + 1, :] = field[(i + 1) * cols - 1 : (i + 1) * cols, BE]
            hew_send[ph, 1, i : i + 1, :] = field[i * cols : i * cols + 1, BW]
        start_copies(halo_copies(ph)[2:4])

    def fold(x):
        return jnp.sum(x.reshape(-1, 8, x.shape[-1]), axis=0)

    def lanes(x):
        total = x[:, :edge]
        for b in range(1, x.shape[1] // edge):
            total = total + x[:, b * edge : (b + 1) * edge]
        return total

    def jump(field, i, b, hs, hn, hw, he):
        r = rowslice(i)
        if b == 0:
            other = jnp.where(first, hw[i : i + 1, :], pltpu.roll(field[r, BE], 1, 0))
            return jnp.where(no_w, 0.0, field[r, BW] - other)
        if b == 1:
            other = jnp.where(final, he[i : i + 1, :], pltpu.roll(field[r, BW], cols - 1, 0))
            return field[r, BE] - other
        if b == 2:
            if i == 0:
                return (field[r, BS] - hs) * keep_s
            return field[r, BS] - field[rowslice(i - 1), BN]
        if i == rows - 1:
            return field[r, BN] - hn
        return field[r, BN] - field[rowslice(i + 1), BS]

    def weight(i, b):
        if b == 1:
            return w_east
        if b == 3 and i == rows - 1:
            return w_north
        return 0.5

    def everywhere(slots):
        part = jnp.sum(slots, axis=0)
        return jnp.sum(jnp.sum(part, axis=1, keepdims=True), axis=0, keepdims=True)

    rk = lax.broadcasted_iota(jnp.int32, (16, ext), 0) % 4
    rk_c = lax.broadcasted_iota(jnp.int32, (16, ncoarse), 0) % 4

    def step_length(it):
        wait_all(cv_slots.at[it, pl.ds(0, n - 1)], a_rsem.at[3 * it + 2])
        curvature = everywhere(cv_slots[it]) + scal[CC, 0:1, 0:1]
        scal[ALPHA] = scal[RZ] / curvature

    def advance():
        alpha = scal[ALPHA, 0:1, :]
        for b in range(4):
            bs = slice(b * edge, (b + 1) * edge)
            res[:, bs] = res[:, bs] - alpha * app[:, bs]
            lam[:, bs] = lam[:, bs] + alpha * dirn[:, bs]

    def take_rz(it, which):
        wait_all(rz_slots.at[it, pl.ds(0, n - 1)], a_rsem.at[3 * it])
        rz_now = jnp.broadcast_to(everywhere(rz_slots[it]), (8, edge))
        scal[which] = rz_now / scal[RZ]
        scal[RZ] = rz_now

    loads[0].wait()
    split_matrices(sdir_v, 0)
    loads[1].wait()
    for i in range(rows):
        for b in range(4):
            set_operand(i, b, weight(i, b) * res[rowslice(i), b * edge : (b + 1) * edge])
    pl.semaphore_wait(barrier, n - 1)
    start_copies(info_copies())
    send_all(None, ginv.at[me], 3 * ITERS)
    WE, SN = slice(0, 2 * edge), slice(2 * edge, 4 * edge)

    def both(x):
        return jnp.concatenate([x, x], axis=1)

    def body(it, carry):
        pa, pb = 2 * it, 2 * it + 1
        new = product(0, 1)

        @pl.when(it == 0)
        def _():
            scal[ALPHA] = jnp.full((8, edge), -1.0, F32)

        @pl.when(it > 0)
        def _():
            step_length(it - 1)

        alpha2 = both(scal[ALPHA, 0:1, :])
        s_f[:, SN] = s_f[:, SN] - alpha2 * new
        send_ns(pa, s_f)
        s_f[:, WE] = s_f[:, WE] - alpha2 * product(0, 0)
        send_ew(pa, s_f)

        @pl.when(it > 0)
        def _():
            advance()

        acc = jnp.zeros((8, edge), F32)
        for i in range(rows):
            for b in range(4):
                bs = slice(b * edge, (b + 1) * edge)
                acc = acc + fold(weight(i, b) * res[rowslice(i), bs] * s_f[rowslice(i), bs])
        rz_slots[it, me] = acc
        send_all(None, rz_slots.at[it, me], 3 * it)

        @pl.when(it == 0)
        def _():
            loads[3].wait()
            split_matrices(sinv_v, 1)
            wait_recv(info_copies())
            coarse_tables()
            loads[2].wait()
            loads[4].wait()
            take_rz(it, EARLY)
            scal[LATE] = jnp.zeros((8, edge), F32)

        @pl.when(it > 0)
        def _():
            scal[EARLY] = jnp.zeros((8, edge), F32)

        early = scal[EARLY, 0:1, :]

        def towards(b, hs, hn, hw, he):
            bs = slice(b * edge, (b + 1) * edge)
            for i in range(rows):
                w = weight(i, b) * jump(s_f, i, b, hs, hn, hw, he) + early * dirn[rowslice(i), bs]
                app[rowslice(i), bs] = w
                set_operand(i, b, w)

        wait_recv(halo_copies(pa)[0:2])
        hs, hn = hns_recv[pa, 0], hns_recv[pa, 1]
        towards(2, hs, hn, None, None)
        towards(3, hs, hn, None, None)
        wait_recv(halo_copies(pa)[2:4])
        hw, he = hew_recv[pa, 0], hew_recv[pa, 1]
        towards(0, None, None, hw, he)
        towards(1, None, None, hw, he)
        d_hi, d_lo = split2(app[...])
        terms = dot(s_hi, d_hi, NT) + (dot(s_lo, d_hi, NT) + dot(s_hi, d_lo, NT))
        terms = terms * sel[:, 0:cells]
        stack = jnp.concatenate(split3(terms), axis=0).astype(BF16)
        load = jnp.zeros((16, ncoarse), F32)
        for k in range(4):
            r = dot(stack, oht[k, :, 0:cells], NT)
            load = load + jnp.where(rk_c == k, r[0:16] + r[16:32] + r[32:48], 0.0)
        co_slots[it, me] = load[0:8] + load[8:16]
        send_all(None, co_slots.at[it, me], 3 * it + 1)
        f_f[:, SN] = product(1, 1)
        send_ns(pb, f_f)
        f_f[:, WE] = product(1, 0)
        send_ew(pb, f_f)

        @pl.when(it > 0)
        def _():
            take_rz(it, LATE)

        late = scal[LATE, 0:1, :]
        acc = jnp.zeros((8, edge), F32)
        for b in range(4):
            bs = slice(b * edge, (b + 1) * edge)
            d = app[:, bs] + late * dirn[:, bs]
            q = f_f[:, bs] + late * p_f[:, bs]
            dirn[:, bs] = d
            p_f[:, bs] = q
            acc = acc + fold(d * q)
        cv_slots[it, me] = acc
        send_all(None, cv_slots.at[it, me], 3 * it + 2)

        @pl.when(it == 0)
        def _():
            wait_all(ginv.at[pl.ds(0, n - 1)], a_rsem.at[3 * ITERS])

        wait_all(co_slots.at[it, pl.ds(0, n - 1)], a_rsem.at[3 * it + 1])
        rhs = jnp.sum(jnp.sum(co_slots[it], axis=0), axis=0, keepdims=True)
        rhs = jnp.broadcast_to(rhs, (8, ncoarse)) + scal[LATE, :, 0:1] * crhs[...]
        crhs[...] = rhs
        sol = lax.dot_general(
            rhs, ginv[...].reshape(ncoarse, ncoarse), NT, precision=HIGHEST,
            preferred_element_type=F32,
        )
        scal[CC] = jnp.broadcast_to(jnp.sum(sol * rhs, axis=1, keepdims=True), (8, edge))
        hi, mid, lo = split3(sol)
        srow = lax.broadcasted_iota(jnp.int32, (8, ncoarse), 0)
        lhs = jnp.where(srow == 0, hi, jnp.where(srow == 1, mid, jnp.where(srow == 2, lo, 0.0)))
        lhs = jnp.concatenate([lhs, jnp.zeros_like(lhs)], axis=0).astype(BF16)
        vals = jnp.zeros((16, ext), F32)
        for k in range(4):
            cv = jnp.sum(dot(lhs, oht[k]), axis=0, keepdims=True)
            vals = jnp.where(rk == k, cv, vals)
        a_hi, a_lo = split2(vals * sel[...])
        a_st = jnp.concatenate([a_hi, a_lo, a_hi], axis=0)
        f_f[...] = p_f[...] + dot(a_st[:, 0:cells], shape_st[...], TN)
        add_s = dot(a_st[:, B_S : B_S + cols], shape_st[:, BN], TN)
        add_n = dot(a_st[:, B_N : B_N + cols], shape_st[:, BS], TN)
        add_w = dot(a_st[:, B_W : B_W + cols], shape_st[:, BE], TN)
        add_e = dot(a_st[:, B_E : B_E + cols], shape_st[:, BW], TN)
        wait_recv(halo_copies(pb))
        for k in range(2):
            hp_ns[k] = hns_recv[pb, k] + late * hp_ns[k]
            hp_ew[k] = hew_recv[pb, k] + late * hp_ew[k]
        hs, hn = hp_ns[0] + add_s, hp_ns[1] + add_n
        hw, he = hp_ew[0] + add_w[0:8], hp_ew[1] + add_e[0:8]
        for i in range(rows):
            for b in range(4):
                bs = slice(b * edge, (b + 1) * edge)
                x = jump(f_f, i, b, hs, hn, hw, he)
                app[rowslice(i), bs] = x
                set_operand(i, b, weight(i, b) * x)
        return carry

    lax.fori_loop(0, ITERS, body, 0)
    step_length(ITERS - 1)
    advance()

    wait_send(info_copies())
    wait_all(ginv.at[pl.ds(0, n - 1)], a_ssem.at[3 * ITERS])
    for it in range(ITERS):
        wait_send(halo_copies(2 * it))
        wait_send(halo_copies(2 * it + 1))
        wait_all(rz_slots.at[it, pl.ds(0, n - 1)], a_ssem.at[3 * it])
        wait_all(co_slots.at[it, pl.ds(0, n - 1)], a_ssem.at[3 * it + 1])
        wait_all(cv_slots.at[it, pl.ds(0, n - 1)], a_ssem.at[3 * it + 2])


def on_device(
    lam_start, resid_start, dirn_start, rz_start, pattern, corners,
    schur_inv, schur_dirichlet, corner_shape, coarse_inv,
):
    rows, cols, dof = lam_start.shape
    edge = dof // 4
    npat = schur_inv.shape[0]
    ncoarse = coarse_inv.shape[1]
    nw, nf, npl = lax.axis_size("warp"), lax.axis_size("weft"), lax.axis_size("ply")
    n = nw * nf * npl
    cells = rows * cols
    ext = cells + 4 * cols
    vmem = pl.BlockSpec(memory_space=pltpu.VMEM)
    hbm = pl.BlockSpec(memory_space=pltpu.HBM)
    out = pltpu.VMEM((cells, dof), F32)
    V = pltpu.VMEM
    D = pltpu.SemaphoreType.DMA
    limit = 121 * 512 * 1024
    outs = pl.pallas_call(
        functools.partial(kernel, nw, nf, npl, rows, cols, edge, npat, ncoarse),
        out_shape=(out, out, out),
        in_specs=[hbm] * 3 + [vmem] * 3 + [hbm] * 2 + [vmem] * 2,
        out_specs=(vmem, vmem, vmem),
        scratch_shapes=[
            V((npat, dof, dof), F32),
            V((npat, dof, dof), F32),
            V((cells, dof), F32),
            V((cells, dof), F32),
            V((cells, dof), F32),
            V((cells, dof), F32),
            V((2, cols, edge), F32),
            V((2, 8, edge), F32),
            V((5, 8, edge), F32),
            V((8, ncoarse), F32),
            V((2, npat * dof, dof), BF16),
            V((2, npat * dof, dof), BF16),
            V((cells, npat * dof), BF16),
            V((cells, npat * dof), BF16),
            V((npat, cells, edge), BF16),
            V((8, ext), F32),
            V((4, 8, cols), F32),
            V((4, ncoarse, ext), BF16),
            V((16, ext), F32),
            V((16, dof), F32),
            V((48, dof), BF16),
            V((n, ncoarse // n, ncoarse), F32),
            V((ITERS, n, 8, edge), F32),
            V((ITERS, n, 8, edge), F32),
            V((ITERS, n, 8, ncoarse), F32),
            V((2 * ITERS, 2, cols, edge), F32),
            V((2 * ITERS, 2, cols, edge), F32),
            V((2 * ITERS, 2, 8, edge), F32),
            V((2 * ITERS, 2, 8, edge), F32),
            D((2 * ITERS, 4)),
            D((2 * ITERS, 4)),
            D((4,)),
            D((4,)),
            D((3 * ITERS + 1,)),
            D((3 * ITERS + 1,)),
            D((5,)),
        ],
        compiler_params=pltpu.CompilerParams(
            collective_id=0, has_side_effects=True, vmem_limit_bytes=limit
        ),
    )(
        lam_start.reshape(cells, dof), resid_start.reshape(cells, dof),
        dirn_start.reshape(cells, dof), rz_start.reshape(1, 1), pattern, corners,
        schur_inv, schur_dirichlet, corner_shape, coarse_inv,
    )
    return tuple(o.reshape(rows, cols, dof) for o in outs)


def solution(mesh):
    field = P(("parts", "warp", "ply"), "weft", None)
    return jax.shard_map(
        on_device,
        mesh=mesh,
        in_specs=(
            field, field, field,
            P("parts"),
            P(("parts", "warp", "ply"), "weft"),
            P(None, ("parts", "warp", "ply"), "weft"),
            P(), P(), P(),
            P(("parts", "warp", "weft", "ply"), None),
        ),
        out_specs=(field, field, field),
        check_vma=False,
    )
```

```python
import functools

import jax
import jax.numpy as jnp
from jax import lax
from jax.experimental import pallas as pl
from jax.experimental.pallas import tpu as pltpu
from jax.sharding import PartitionSpec as P

ITERS = 3
HIGHEST = lax.Precision.HIGHEST
F32 = jnp.float32
BF16 = jnp.bfloat16
MESH = pl.DeviceIdType.MESH
NN = (((1,), (0,)), ((), ()))
NT = (((1,), (1,)), ((), ()))
TN = (((0,), (0,)), ((), ()))


def dot(a, b, dims=NN):
    return lax.dot_general(a, b, dims, preferred_element_type=F32)


def split2(x):
    hi = x.astype(BF16)
    return hi, (x - hi.astype(F32)).astype(BF16)


def split3(x):
    hi = x.astype(BF16).astype(F32)
    rest = x - hi
    mid = rest.astype(BF16).astype(F32)
    return hi, mid, rest - mid


def kernel(
    nw, nf, npl, rows, cols, edge, npat, ncoarse,
    lam_in, res_in, dir_in, rz_in, pat, cor, sinv, sdir, shp, cinv,
    lam, res, dirn,
    sdir_v, sinv_v, s_f, p_f, f_f, app, hp_ns, hp_ew, scal, crhs,
    m_hi, m_lo, x_hi, x_lo, masks, info, infosend, oht, sel, shape_f, shape_st,
    ginv, rz_slots, cv_slots, co_slots,
    hns_send, hns_recv, hew_send, hew_recv,
    h_ssem, h_rsem, i_ssem, i_rsem, a_ssem, a_rsem, l_sem,
):
    n = nw * nf * npl
    cells = rows * cols
    dof = 4 * edge
    warp, weft, ply = lax.axis_index("warp"), lax.axis_index("weft"), lax.axis_index("ply")
    me = (warp * nf + weft) * npl + ply
    tile = warp * npl + ply
    ntile = nw * npl
    has_n, has_s = tile < ntile - 1, tile > 0
    has_e, has_w = weft < nf - 1, weft > 0
    north = {"warp": (tile + 1) // npl, "ply": (tile + 1) % npl, "weft": weft}
    south = {"warp": (tile + ntile - 1) // npl % nw, "ply": (tile + npl - 1) % npl, "weft": weft}
    east = {"warp": warp, "ply": ply, "weft": weft + 1}
    west = {"warp": warp, "ply": ply, "weft": weft - 1}

    def peer(t):
        other = lax.rem(me + t, n)
        return {"warp": other // (nf * npl), "weft": other // npl % nf, "ply": other % npl}

    RZ, ALPHA, EARLY, LATE, CC = range(5)
    B_S, B_N, B_W, B_E = (cells + k * cols for k in range(4))

    barrier = pltpu.get_barrier_semaphore()

    def greet(t, c):
        pl.semaphore_signal(barrier, inc=1, device_id=peer(t), device_id_type=MESH)
        return c

    loads = [
        pltpu.make_async_copy(src, dst, l_sem.at[k])
        for k, (src, dst) in enumerate(
            ((sdir, sdir_v), (res_in, res), (dir_in, dirn), (sinv, sinv_v), (lam_in, lam))
        )
    ]
    for load in loads:
        load.start()

    for k in range(4):
        for i in range(rows):
            info[k : k + 1, i * cols : (i + 1) * cols] = cor[k, i : i + 1, :].astype(F32)
    for i in range(rows):
        info[4:5, i * cols : (i + 1) * cols] = pat[i : i + 1, :].astype(F32)
    info[5:8, 0:cells] = jnp.zeros((3, cells), F32)
    for there, lane in ((has_s, B_S), (has_n, B_N), (has_w, B_W), (has_e, B_E)):
        @pl.when(jnp.logical_not(there))
        def _():
            info[:, lane : lane + cols] = jnp.full((8, cols), -1.0, F32)
    for there, k in ((has_s, 0), (has_n, 1)):
        @pl.when(jnp.logical_not(there))
        def _():
            hns_recv[:, k] = jnp.zeros((2 * ITERS, cols, edge), F32)
    for there, k in ((has_w, 0), (has_e, 1)):
        @pl.when(jnp.logical_not(there))
        def _():
            hew_recv[:, k] = jnp.zeros((2 * ITERS, 8, edge), F32)
    own = info[:, 0:cells]
    infosend[0] = own[:, (rows - 1) * cols :]
    infosend[1] = own[:, :cols]
    cell_i = lax.broadcasted_iota(jnp.int32, (cells, cols), 0)
    lane_i = lax.broadcasted_iota(jnp.int32, (cells, cols), 1)
    for slot, j in ((2, cols - 1), (3, 0)):
        pick = jnp.where(cell_i == lane_i * cols + j, 1.0, 0.0).astype(F32)
        infosend[slot] = lax.dot_general(
            own, pick, NN, precision=HIGHEST, preferred_element_type=F32
        )
    ginv[me] = cinv[...]
    lax.fori_loop(1, n, greet, 0)

    def send_all(ref, src, which):
        def one(t, c):
            pltpu.make_async_remote_copy(
                src_ref=src, dst_ref=src, send_sem=a_ssem.at[which], recv_sem=a_rsem.at[which],
                device_id=peer(t), device_id_type=MESH,
            ).start()
            return c

        lax.fori_loop(1, n, one, 0)

    def wait_all(ref, sem):
        pltpu.make_async_copy(ref, ref, sem).wait()

    def put(src, dst, ssem, rsem, to):
        return pltpu.make_async_remote_copy(
            src_ref=src, dst_ref=dst, send_sem=ssem, recv_sem=rsem,
            device_id=to, device_id_type=MESH,
        )

    def info_copies():
        return (
            (has_n, has_s, put(infosend.at[0], info.at[:, B_S : B_S + cols], i_ssem.at[0], i_rsem.at[0], north)),
            (has_s, has_n, put(infosend.at[1], info.at[:, B_N : B_N + cols], i_ssem.at[1], i_rsem.at[1], south)),
            (has_e, has_w, put(infosend.at[2], info.at[:, B_W : B_W + cols], i_ssem.at[2], i_rsem.at[2], east)),
            (has_w, has_e, put(infosend.at[3], info.at[:, B_E : B_E + cols], i_ssem.at[3], i_rsem.at[3], west)),
        )

    def halo_copies(ph):
        return (
            (has_n, has_s, put(hns_send.at[ph, 0], hns_recv.at[ph, 0], h_ssem.at[ph, 0], h_rsem.at[ph, 0], north)),
            (has_s, has_n, put(hns_send.at[ph, 1], hns_recv.at[ph, 1], h_ssem.at[ph, 1], h_rsem.at[ph, 1], south)),
            (has_e, has_w, put(hew_send.at[ph, 0], hew_recv.at[ph, 0], h_ssem.at[ph, 2], h_rsem.at[ph, 2], east)),
            (has_w, has_e, put(hew_send.at[ph, 1], hew_recv.at[ph, 1], h_ssem.at[ph, 3], h_rsem.at[ph, 3], west)),
        )

    def start_copies(copies):
        for out, _, copy in copies:
            @pl.when(out)
            def _(copy=copy):
                copy.start()

    def wait_recv(copies):
        for _, came, copy in copies:
            @pl.when(came)
            def _(copy=copy):
                copy.wait_recv()

    def wait_send(copies):
        for out, _, copy in copies:
            @pl.when(out)
            def _(copy=copy):
                copy.wait_send()

    def split_matrices(src, which):
        for p in range(npat):
            hi, lo = split2(src[p])
            m_hi[which, p * dof : (p + 1) * dof, :] = hi
            m_lo[which, p * dof : (p + 1) * dof, :] = lo

    prow = lax.broadcasted_iota(jnp.int32, (8, cells), 0).astype(F32)
    onehot = jnp.where(prow == own[4:5, :], 1.0, 0.0).astype(F32)
    for p in range(npat):
        spread_p = jnp.where(lax.broadcasted_iota(jnp.int32, (8, edge), 0) == p, 1.0, 0.0)
        masks[p] = dot(onehot.astype(BF16), spread_p.astype(BF16), TN).astype(BF16)
    shape_f[...] = jnp.zeros_like(shape_f)
    for p in range(npat):
        shape_f[4 * p : 4 * p + 4, :] = shp[p]
    s_hi, s_lo = split2(shape_f[...])
    shape_st[0:16, :] = s_hi
    shape_st[16:32, :] = s_hi
    shape_st[32:48, :] = s_lo
    for ref in (s_f, p_f, hp_ns, hp_ew, crhs):
        ref[...] = jnp.zeros_like(ref)
    scal[RZ] = jnp.broadcast_to(rz_in[...], (8, edge))
    ext = cells + 4 * cols

    def coarse_tables():
        row_k = lax.broadcasted_iota(jnp.int32, (16, ext), 0)
        sel[...] = jnp.where((row_k // 4).astype(F32) == info[4:5, :], 1.0, 0.0)
        coarse_row = lax.broadcasted_iota(jnp.int32, (ncoarse, ext), 0).astype(F32)
        for k in range(4):
            oht[k] = jnp.where(coarse_row == info[k : k + 1, :], 1.0, 0.0).astype(BF16)

    sub = lax.broadcasted_iota(jnp.int32, (cols, edge), 0)
    first, final = sub == 0, sub == cols - 1
    w_east = jnp.where(final & jnp.logical_not(has_e), 1.0, 0.5)
    no_w = first & jnp.logical_not(has_w)
    w_north = jnp.where(has_n, 0.5, 1.0)
    keep_s = jnp.where(has_s, 1.0, 0.0)
    BW, BE, BS, BN = (slice(b * edge, (b + 1) * edge) for b in range(4))

    def rowslice(i):
        return slice(i * cols, (i + 1) * cols)

    def set_operand(i, b, x):
        hi, lo = split2(x)
        for p in range(npat):
            m = masks[p, rowslice(i), :]
            x_hi[rowslice(i), p * dof + b * edge : p * dof + (b + 1) * edge] = hi * m
            x_lo[rowslice(i), p * dof + b * edge : p * dof + (b + 1) * edge] = lo * m

    def product(which):
        xh = x_hi[...]
        mh = m_hi[which]
        return dot(xh, mh) + (dot(x_lo[...], mh) + dot(xh, m_lo[which]))

    def send_ns(ph, field):
        hns_send[ph, 0] = field[rowslice(rows - 1), BN]
        hns_send[ph, 1] = field[rowslice(0), BS]
        start_copies(halo_copies(ph)[0:2])

    def send_ew(ph, field):
        for i in range(rows):
            hew_send[ph, 0, i : i + 1, :] = field[(i + 1) * cols - 1 : (i + 1) * cols, BE]
            hew_send[ph, 1, i : i + 1, :] = field[i * cols : i * cols + 1, BW]
        start_copies(halo_copies(ph)[2:4])

    def fold(x):
        return jnp.sum(x.reshape(-1, 8, x.shape[-1]), axis=0)

    def lanes(x):
        total = x[:, :edge]
        for b in range(1, x.shape[1] // edge):
            total = total + x[:, b * edge : (b + 1) * edge]
        return total

    def jump(field, i, b, hs, hn, hw, he):
        r = rowslice(i)
        if b == 0:
            other = jnp.where(first, hw[i : i + 1, :], pltpu.roll(field[r, BE], 1, 0))
            return jnp.where(no_w, 0.0, field[r, BW] - other)
        if b == 1:
            other = jnp.where(final, he[i : i + 1, :], pltpu.roll(field[r, BW], cols - 1, 0))
            return field[r, BE] - other
        if b == 2:
            if i == 0:
                return (field[r, BS] - hs) * keep_s
            return field[r, BS] - field[rowslice(i - 1), BN]
        if i == rows - 1:
            return field[r, BN] - hn
        return field[r, BN] - field[rowslice(i + 1), BS]

    def weight(i, b):
        if b == 1:
            return w_east
        if b == 3 and i == rows - 1:
            return w_north
        return 0.5

    def everywhere(slots):
        part = jnp.sum(slots, axis=0)
        return jnp.sum(jnp.sum(part, axis=1, keepdims=True), axis=0, keepdims=True)

    rk = lax.broadcasted_iota(jnp.int32, (16, ext), 0) % 4
    rk_c = lax.broadcasted_iota(jnp.int32, (16, ncoarse), 0) % 4

    def step_length(it):
        wait_all(cv_slots.at[it, pl.ds(0, n - 1)], a_rsem.at[3 * it + 2])
        curvature = everywhere(cv_slots[it]) + scal[CC, 0:1, 0:1]
        scal[ALPHA] = scal[RZ] / curvature

    def advance():
        alpha = scal[ALPHA, 0:1, :]
        for b in range(4):
            bs = slice(b * edge, (b + 1) * edge)
            res[:, bs] = res[:, bs] - alpha * app[:, bs]
            lam[:, bs] = lam[:, bs] + alpha * dirn[:, bs]

    def take_rz(it, which):
        wait_all(rz_slots.at[it, pl.ds(0, n - 1)], a_rsem.at[3 * it])
        rz_now = jnp.broadcast_to(everywhere(rz_slots[it]), (8, edge))
        scal[which] = rz_now / scal[RZ]
        scal[RZ] = rz_now

    loads[0].wait()
    split_matrices(sdir_v, 0)
    loads[1].wait()
    for i in range(rows):
        for b in range(4):
            set_operand(i, b, weight(i, b) * res[rowslice(i), b * edge : (b + 1) * edge])
    pl.semaphore_wait(barrier, n - 1)
    start_copies(info_copies())
    send_all(None, ginv.at[me], 3 * ITERS)
    WE, SN = slice(0, 2 * edge), slice(2 * edge, 4 * edge)

    def both(x):
        return jnp.concatenate([x, x], axis=1)

    def body(it, carry):
        pa, pb = 2 * it, 2 * it + 1
        new = product(0)

        @pl.when(it == 0)
        def _():
            scal[ALPHA] = jnp.full((8, edge), -1.0, F32)

        @pl.when(it > 0)
        def _():
            step_length(it - 1)

        alpha2 = both(scal[ALPHA, 0:1, :])
        s_f[...] = s_f[...] - both(alpha2) * new
        send_ns(pa, s_f)
        send_ew(pa, s_f)

        @pl.when(it > 0)
        def _():
            advance()

        acc = jnp.zeros((8, edge), F32)
        for i in range(rows):
            for b in range(4):
                bs = slice(b * edge, (b + 1) * edge)
                acc = acc + fold(weight(i, b) * res[rowslice(i), bs] * s_f[rowslice(i), bs])
        rz_slots[it, me] = acc
        send_all(None, rz_slots.at[it, me], 3 * it)

        @pl.when(it == 0)
        def _():
            loads[3].wait()
            split_matrices(sinv_v, 1)
            wait_recv(info_copies())
            coarse_tables()
            loads[2].wait()
            loads[4].wait()
            take_rz(it, EARLY)
            scal[LATE] = jnp.zeros((8, edge), F32)

        @pl.when(it > 0)
        def _():
            scal[EARLY] = jnp.zeros((8, edge), F32)

        early = scal[EARLY, 0:1, :]

        def towards(b, hs, hn, hw, he):
            bs = slice(b * edge, (b + 1) * edge)
            for i in range(rows):
                w = weight(i, b) * jump(s_f, i, b, hs, hn, hw, he) + early * dirn[rowslice(i), bs]
                app[rowslice(i), bs] = w
                set_operand(i, b, w)

        wait_recv(halo_copies(pa)[0:2])
        hs, hn = hns_recv[pa, 0], hns_recv[pa, 1]
        towards(2, hs, hn, None, None)
        towards(3, hs, hn, None, None)
        wait_recv(halo_copies(pa)[2:4])
        hw, he = hew_recv[pa, 0], hew_recv[pa, 1]
        towards(0, None, None, hw, he)
        towards(1, None, None, hw, he)
        d_hi, d_lo = split2(app[...])
        terms = dot(s_hi, d_hi, NT) + (dot(s_lo, d_hi, NT) + dot(s_hi, d_lo, NT))
        terms = terms * sel[:, 0:cells]
        stack = jnp.concatenate(split3(terms), axis=0).astype(BF16)
        load = jnp.zeros((16, ncoarse), F32)
        for k in range(4):
            r = dot(stack, oht[k, :, 0:cells], NT)
            load = load + jnp.where(rk_c == k, r[0:16] + r[16:32] + r[32:48], 0.0)
        co_slots[it, me] = load[0:8] + load[8:16]
        send_all(None, co_slots.at[it, me], 3 * it + 1)
        f_f[...] = product(1)
        send_ns(pb, f_f)
        send_ew(pb, f_f)

        @pl.when(it > 0)
        def _():
            take_rz(it, LATE)

        late = scal[LATE, 0:1, :]
        acc = jnp.zeros((8, edge), F32)
        for b in range(4):
            bs = slice(b * edge, (b + 1) * edge)
            d = app[:, bs] + late * dirn[:, bs]
            q = f_f[:, bs] + late * p_f[:, bs]
            dirn[:, bs] = d
            p_f[:, bs] = q
            acc = acc + fold(d * q)
        cv_slots[it, me] = acc
        send_all(None, cv_slots.at[it, me], 3 * it + 2)

        @pl.when(it == 0)
        def _():
            wait_all(ginv.at[pl.ds(0, n - 1)], a_rsem.at[3 * ITERS])

        wait_all(co_slots.at[it, pl.ds(0, n - 1)], a_rsem.at[3 * it + 1])
        rhs = jnp.sum(jnp.sum(co_slots[it], axis=0), axis=0, keepdims=True)
        rhs = jnp.broadcast_to(rhs, (8, ncoarse)) + scal[LATE, :, 0:1] * crhs[...]
        crhs[...] = rhs
        sol = lax.dot_general(
            rhs, ginv[...].reshape(ncoarse, ncoarse), NT, precision=HIGHEST,
            preferred_element_type=F32,
        )
        scal[CC] = jnp.broadcast_to(jnp.sum(sol * rhs, axis=1, keepdims=True), (8, edge))
        hi, mid, lo = split3(sol)
        srow = lax.broadcasted_iota(jnp.int32, (8, ncoarse), 0)
        lhs = jnp.where(srow == 0, hi, jnp.where(srow == 1, mid, jnp.where(srow == 2, lo, 0.0)))
        lhs = jnp.concatenate([lhs, jnp.zeros_like(lhs)], axis=0).astype(BF16)
        vals = jnp.zeros((16, ext), F32)
        for k in range(4):
            cv = jnp.sum(dot(lhs, oht[k]), axis=0, keepdims=True)
            vals = jnp.where(rk == k, cv, vals)
        a_hi, a_lo = split2(vals * sel[...])
        a_st = jnp.concatenate([a_hi, a_lo, a_hi], axis=0)
        f_f[...] = p_f[...] + dot(a_st[:, 0:cells], shape_st[...], TN)
        add_s = dot(a_st[:, B_S : B_S + cols], shape_st[:, BN], TN)
        add_n = dot(a_st[:, B_N : B_N + cols], shape_st[:, BS], TN)
        add_w = dot(a_st[:, B_W : B_W + cols], shape_st[:, BE], TN)
        add_e = dot(a_st[:, B_E : B_E + cols], shape_st[:, BW], TN)
        wait_recv(halo_copies(pb))
        for k in range(2):
            hp_ns[k] = hns_recv[pb, k] + late * hp_ns[k]
            hp_ew[k] = hew_recv[pb, k] + late * hp_ew[k]
        hs, hn = hp_ns[0] + add_s, hp_ns[1] + add_n
        hw, he = hp_ew[0] + add_w[0:8], hp_ew[1] + add_e[0:8]
        for i in range(rows):
            for b in range(4):
                bs = slice(b * edge, (b + 1) * edge)
                x = jump(f_f, i, b, hs, hn, hw, he)
                app[rowslice(i), bs] = x
                set_operand(i, b, weight(i, b) * x)
        return carry

    lax.fori_loop(0, ITERS, body, 0)
    step_length(ITERS - 1)
    advance()

    wait_send(info_copies())
    wait_all(ginv.at[pl.ds(0, n - 1)], a_ssem.at[3 * ITERS])
    for it in range(ITERS):
        wait_send(halo_copies(2 * it))
        wait_send(halo_copies(2 * it + 1))
        wait_all(rz_slots.at[it, pl.ds(0, n - 1)], a_ssem.at[3 * it])
        wait_all(co_slots.at[it, pl.ds(0, n - 1)], a_ssem.at[3 * it + 1])
        wait_all(cv_slots.at[it, pl.ds(0, n - 1)], a_ssem.at[3 * it + 2])


def on_device(
    lam_start, resid_start, dirn_start, rz_start, pattern, corners,
    schur_inv, schur_dirichlet, corner_shape, coarse_inv,
):
    rows, cols, dof = lam_start.shape
    edge = dof // 4
    npat = schur_inv.shape[0]
    ncoarse = coarse_inv.shape[1]
    nw, nf, npl = lax.axis_size("warp"), lax.axis_size("weft"), lax.axis_size("ply")
    n = nw * nf * npl
    cells = rows * cols
    ext = cells + 4 * cols
    vmem = pl.BlockSpec(memory_space=pltpu.VMEM)
    hbm = pl.BlockSpec(memory_space=pltpu.HBM)
    out = pltpu.VMEM((cells, dof), F32)
    V = pltpu.VMEM
    D = pltpu.SemaphoreType.DMA
    limit = 121 * 512 * 1024
    outs = pl.pallas_call(
        functools.partial(kernel, nw, nf, npl, rows, cols, edge, npat, ncoarse),
        out_shape=(out, out, out),
        in_specs=[hbm] * 3 + [vmem] * 3 + [hbm] * 2 + [vmem] * 2,
        out_specs=(vmem, vmem, vmem),
        scratch_shapes=[
            V((npat, dof, dof), F32),
            V((npat, dof, dof), F32),
            V((cells, dof), F32),
            V((cells, dof), F32),
            V((cells, dof), F32),
            V((cells, dof), F32),
            V((2, cols, edge), F32),
            V((2, 8, edge), F32),
            V((5, 8, edge), F32),
            V((8, ncoarse), F32),
            V((2, npat * dof, dof), BF16),
            V((2, npat * dof, dof), BF16),
            V((cells, npat * dof), BF16),
            V((cells, npat * dof), BF16),
            V((npat, cells, edge), BF16),
            V((8, ext), F32),
            V((4, 8, cols), F32),
            V((4, ncoarse, ext), BF16),
            V((16, ext), F32),
            V((16, dof), F32),
            V((48, dof), BF16),
            V((n, ncoarse // n, ncoarse), F32),
            V((ITERS, n, 8, edge), F32),
            V((ITERS, n, 8, edge), F32),
            V((ITERS, n, 8, ncoarse), F32),
            V((2 * ITERS, 2, cols, edge), F32),
            V((2 * ITERS, 2, cols, edge), F32),
            V((2 * ITERS, 2, 8, edge), F32),
            V((2 * ITERS, 2, 8, edge), F32),
            D((2 * ITERS, 4)),
            D((2 * ITERS, 4)),
            D((4,)),
            D((4,)),
            D((3 * ITERS + 1,)),
            D((3 * ITERS + 1,)),
            D((5,)),
        ],
        compiler_params=pltpu.CompilerParams(
            collective_id=0, has_side_effects=True, vmem_limit_bytes=limit
        ),
    )(
        lam_start.reshape(cells, dof), resid_start.reshape(cells, dof),
        dirn_start.reshape(cells, dof), rz_start.reshape(1, 1), pattern, corners,
        schur_inv, schur_dirichlet, corner_shape, coarse_inv,
    )
    return tuple(o.reshape(rows, cols, dof) for o in outs)


def solution(mesh):
    field = P(("parts", "warp", "ply"), "weft", None)
    return jax.shard_map(
        on_device,
        mesh=mesh,
        in_specs=(
            field, field, field,
            P("parts"),
            P(("parts", "warp", "ply"), "weft"),
            P(None, ("parts", "warp", "ply"), "weft"),
            P(), P(), P(),
            P(("parts", "warp", "weft", "ply"), None),
        ),
        out_specs=(field, field, field),
        check_vma=False,
    )
```
